32 devices in a mesh: row: 4 (over y, core), col: 8 (over z, x).
Axes of the slice: x: 2, y: 2, z: 4, core: 2. Of those that a mesh axis runs over, the one named last changes fastest.
Arguments:
- object_field: float32 [2, 1024, 2048], P(None, 'row', 'col'), may hold values from -4.2 to 4.2
- probe_modes: float32 [2, 8, 256, 256], replicated, may hold values from -1.5 to 1.5
- patterns: float32 [64, 256, 256], P(('row', 'col')), may hold values from 0.3 to 3
- offsets: int32 [2, 64], P(None, ('row', 'col')), may hold values from 0 to 1792, as said below
- counts: int32 [32], P(('row', 'col')), may hold values from 1 to 2, as said below
Outputs:
- new_object: float32 [2, 1024, 2048], P(None, 'row', 'col')
- new_probe: float32 [2, 8, 256, 256], replicated
The draws below stay inside these ranges and needn't reach their ends.
Inputs may be any that keep to these rules, and one draw needn't show every extreme that they name: `offsets`: A slot of the device of tile row r and tile column c has row offset in [r * 256, (r + 1) * 256) and column offset in [c * 256, (c + 1) * 256); every patch lies inside the object. `counts`: A device's live slots are its first ones.
All inputs are finite; a program needn't handle non-finite values.
Results may differ from the reference program's by a relative error of at most 0.0001.
Values sent between devices are 32-bit elements; how exact they have to be, the bound alone decides.
A program may use at most 128 MiB of HBM per device.

```python
import math
import jax
import jax.numpy as jnp
from jax import lax

FRAME = 256
MODES = 8
TILE = 256
SLOTS = 2
HEIGHT = 1024
WIDTH = 2048
POSITIONS = 64
N_ROW = 4
N_COL = 8


def draw_offsets(key, part):
    total = N_ROW * N_COL * SLOTS
    slot_ids = jnp.arange(total, dtype=jnp.int32)
    device_ids = slot_ids // SLOTS
    tile_row = device_ids // N_COL
    tile_col = device_ids % N_COL
    height_all = TILE * N_ROW
    width_all = TILE * N_COL
    limit_row = jnp.minimum(TILE, height_all - FRAME - tile_row * TILE + 1)
    limit_col = jnp.minimum(TILE, width_all - FRAME - tile_col * TILE + 1)
    first_key = jax.random.fold_in(key, 11)
    second_key = jax.random.fold_in(key, 23)
    raw_row = jax.random.randint(first_key, (total,), 0, 1 << 30, dtype=jnp.int32)
    raw_col = jax.random.randint(second_key, (total,), 0, 1 << 30, dtype=jnp.int32)
    row_offset = tile_row * TILE + raw_row % limit_row
    col_offset = tile_col * TILE + raw_col % limit_col
    row_offset = jnp.where(slot_ids == 0, 0, row_offset)
    col_offset = jnp.where(slot_ids == 0, 0, col_offset)
    row_offset = jnp.where(slot_ids == total - 1, height_all - FRAME, row_offset)
    col_offset = jnp.where(slot_ids == total - 1, width_all - FRAME, col_offset)
    return jnp.stack([row_offset, col_offset]).astype(jnp.int32)


def draw_counts(key, part):
    devices_all = N_ROW * N_COL
    fewest = max(1, SLOTS - 1)
    drawn = jax.random.randint(jax.random.fold_in(key, 37), (devices_all,), fewest, SLOTS + 1, dtype=jnp.int32)
    drawn = drawn.at[0].set(SLOTS)
    drawn = drawn.at[devices_all - 1].set(fewest)
    return drawn.astype(jnp.int32)


def levels(own_key, shape, split, least, high):
    def one(dim, shards_of):
        draws = jax.random.uniform(jax.random.fold_in(jax.random.fold_in(own_key, 6), dim), (shards_of,), jnp.float32, least / len(split), high / len(split))
        return jnp.repeat(jnp.exp(draws), shape[dim] // shards_of).reshape((-1,) + (1,) * (len(shape) - dim - 1))

    level = one(*split[0])
    for cut in split[1:]:
        level = level * one(*cut)
    return level


def bell_draw(own_key, extent, scale, limit, shards=(), kind=jnp.bfloat16):
    result = jax.random.normal(own_key, extent, jnp.float32) * scale
    if len(shards) > 0:
        result = levels(own_key, extent, shards, -0.22, 0.18) * result
    return jnp.clip(result, min=-limit, max=limit).astype(kind)


def setup_inputs(seed: int = 0) -> dict:
    seeds = jax.random.split(jax.random.key(seed), 6)
    return {
        "object_field": bell_draw(seeds[0], (2, HEIGHT, WIDTH), 0.7, 4.2, ((1, 4), (2, 8)), jnp.float32),
        "probe_modes": bell_draw(seeds[1], (2, MODES, FRAME, FRAME), 0.25, 1.5, (), jnp.float32),
        "patterns": jnp.clip(jnp.exp(math.log(3.0) - 2.3025851 * jax.random.uniform(seeds[2], (POSITIONS, FRAME, FRAME), jnp.float32) ** levels(seeds[2], (POSITIONS, FRAME, FRAME), ((0, 32),), -0.2, 0.2)), 0.3, 3.0),
        "offsets": draw_offsets(jax.random.fold_in(seeds[5], 71), 0),
        "counts": draw_counts(jax.random.fold_in(seeds[5], 71), 0),
    }


INTENSITY_FLOOR = 0.1
OBJECT_DELTA = 0.5
PROBE_DELTA = 1.0
SMOOTH_WEIGHT = 0.1

def reference(object_field, probe_modes, patterns, offsets, counts):
    float_type = object_field.dtype
    object_now = lax.complex(object_field[0], object_field[1])
    probe_field = lax.complex(probe_modes[0], probe_modes[1])
    probe_power = lax.optimization_barrier(jnp.sum(probe_modes[0] * probe_modes[0] + probe_modes[1] * probe_modes[1], axis=0))

    def visit_position(position, running):
        numerator, illumination, gradient, object_power = running
        position = jnp.asarray(position).astype(jnp.int32)
        row_start = offsets[0, position].astype(jnp.int32)
        col_start = offsets[1, position].astype(jnp.int32)
        live_flag = (position % SLOTS < counts[position // SLOTS]).astype(float_type)
        object_patch = lax.dynamic_slice(object_now, (row_start, col_start), (FRAME, FRAME))
        exit_wave = probe_field * object_patch[None]
        spectrum = jnp.fft.fft2(exit_wave, norm='ortho')
        intensity = lax.optimization_barrier(jnp.sum(jnp.real(spectrum) * jnp.real(spectrum) + jnp.imag(spectrum) * jnp.imag(spectrum), axis=0))
        scale_ratio = patterns[position] / jnp.sqrt(jnp.maximum(intensity, INTENSITY_FLOOR))
        revised = jnp.fft.ifft2(spectrum * scale_ratio[None], norm='ortho')
        difference = (revised - exit_wave) * live_flag
        numer_piece = lax.optimization_barrier(jnp.sum(jnp.conj(probe_field) * difference, axis=0))
        current = lax.dynamic_slice(numerator, (row_start, col_start), (FRAME, FRAME))
        numerator = lax.dynamic_update_slice(numerator, current + numer_piece, (row_start, col_start))
        current_light = lax.dynamic_slice(illumination, (row_start, col_start), (FRAME, FRAME))
        illumination = lax.dynamic_update_slice(illumination, current_light + live_flag * probe_power, (row_start, col_start))
        gradient = gradient + jnp.conj(object_patch)[None] * difference
        patch_power = jnp.real(object_patch) * jnp.real(object_patch) + jnp.imag(object_patch) * jnp.imag(object_patch)
        object_power = object_power + live_flag * patch_power
        return (numerator, illumination, gradient, object_power)
    initial = (jnp.zeros_like(object_now), jnp.zeros((HEIGHT, WIDTH), float_type), jnp.zeros_like(probe_field), jnp.zeros((FRAME, FRAME), float_type))
    numerator, illumination, gradient, object_power = lax.fori_loop(0, POSITIONS, visit_position, initial)
    updated = object_now + numerator / (illumination + OBJECT_DELTA)
    padded = jnp.pad(updated, 1)
    neighbours = padded[2:, 1:-1] + padded[:-2, 1:-1] + padded[1:-1, 2:] + padded[1:-1, :-2]
    smoothed = updated + SMOOTH_WEIGHT * (neighbours - 4.0 * updated)
    probe_next = probe_field + gradient / (object_power + PROBE_DELTA)
    return (jnp.stack([jnp.real(smoothed), jnp.imag(smoothed)]), jnp.stack([jnp.real(probe_next), jnp.imag(probe_next)]))
```

```python
import functools
import math

import jax
import jax.numpy as jnp
import ml_dtypes
import numpy as np
from jax import lax
from jax.experimental import pallas as pl
from jax.experimental.pallas import tpu as pltpu
from jax.sharding import PartitionSpec as P

INTENSITY_FLOOR = 0.1
OBJECT_DELTA = 0.5
PROBE_DELTA = 1.0
SMOOTH_WEIGHT = 0.1
F32 = jnp.float32
BF16 = jnp.bfloat16


def tables(frame):
    half = frame // 2
    n = np.arange(half)
    angle = -2.0 * np.pi * (np.outer(n, n) % half) / half
    c, s = np.cos(angle) / math.sqrt(frame), np.sin(angle) / math.sqrt(frame)
    full = np.block([[c, s], [-s, c]]).astype(np.float32)
    high = full.astype(ml_dtypes.bfloat16)
    low = (full - high.astype(np.float32)).astype(ml_dtypes.bfloat16)
    right_f = np.concatenate([high, high, low], axis=0)
    right_i = np.concatenate([high.T, high.T, low.T], axis=0)
    left_f = np.concatenate([high.T, high.T, low.T], axis=1)
    left_i = np.concatenate([high, high, low], axis=1)
    turn = -2.0 * np.pi * n / frame
    tw = np.stack([np.cos(turn), np.sin(turn)]).astype(np.float32)
    rows = np.broadcast_to(tw[:, None, :], (2, 8, half)).copy()
    cols = np.broadcast_to(tw[:, :, None], (2, half, frame)).copy()
    return right_f, right_i, left_f, left_i, rows, cols


def split(x):
    high = x.astype(BF16)
    return high, (x - high.astype(F32)).astype(BF16)


def right_dot(x, table):
    high, low = split(x)
    return jnp.dot(jnp.concatenate([high, low, high], axis=1), table, preferred_element_type=F32)


def left_dot(table, x):
    high, low = split(x)
    return jnp.dot(table, jnp.concatenate([high, low, high], axis=0), preferred_element_type=F32)


def waves_kernel(
    place, live, own, right, down, diag, probe, amplitude, rf, ri, lf, li, twr, twc,
    totals, grad, power, spectra, ratio, accum,
):
    modes, frame = probe.shape[1], probe.shape[2]
    half = frame // 2
    slots = amplitude.shape[0]
    tile = own.shape[1]
    cat = jnp.concatenate

    for slot in range(slots):
        row, col = place[0, slot], place[1, slot]
        flag = live[slot].astype(F32)
        height, width = 2 * tile, 2 * tile
        patch = []
        for part in range(2):
            whole = cat(
                [cat([own[part], right[part]], axis=1), cat([down[part], diag[part]], axis=1)], axis=0
            )
            whole = pltpu.roll(whole, lax.rem(height - row, height), 0)[:frame]
            patch.append(pltpu.roll(whole, lax.rem(width - col, width), 1)[:, :frame])
        qr, qi = patch
        accum[0], accum[1] = qr, qi
        accum[2] = jnp.zeros((frame, frame), F32)

        @pl.loop(0, modes)
        def _(m):
            qr, qi, pr, pi = accum[0], accum[1], probe[0, m], probe[1, m]
            wr, wi = pr * qr - pi * qi, pr * qi + pi * qr
            c, s = twr[0, 0:1], twr[1, 0:1]
            dr, di = wr[:, :half] - wr[:, half:], wi[:, :half] - wi[:, half:]
            x = cat(
                [
                    cat([wr[:, :half] + wr[:, half:], wi[:, :half] + wi[:, half:]], axis=1),
                    cat([dr * c - di * s, dr * s + di * c], axis=1),
                ],
                axis=0,
            )
            y = right_dot(x, rf[...])
            yr = cat([y[:frame, :half], y[frame:, :half]], axis=1)
            yi = cat([y[:frame, half:], y[frame:, half:]], axis=1)
            c, s = twc[0], twc[1]
            dr, di = yr[:half] - yr[half:], yi[:half] - yi[half:]
            z = cat(
                [
                    cat([yr[:half] + yr[half:], yi[:half] + yi[half:]], axis=0),
                    cat([dr * c - di * s, dr * s + di * c], axis=0),
                ],
                axis=1,
            )
            r = left_dot(lf[...], z)
            spectra[m] = r
            accum[2] += cat(
                [
                    r[:half, :frame] * r[:half, :frame] + r[half:, :frame] * r[half:, :frame],
                    r[:half, frame:] * r[:half, frame:] + r[half:, frame:] * r[half:, frame:],
                ],
                axis=0,
            )

        scale = amplitude[slot] * lax.rsqrt(jnp.maximum(accum[2], INTENSITY_FLOOR))
        ratio[:half, :frame] = scale[:half]
        ratio[half:, :frame] = scale[:half]
        ratio[:half, frame:] = scale[half:]
        ratio[half:, frame:] = scale[half:]
        for part in range(3):
            accum[2 + part] = jnp.zeros((frame, frame), F32)

        @pl.loop(0, modes)
        def _(m):
            r = left_dot(li[...], spectra[m] * ratio[...])
            c, s = twc[0], twc[1]
            er, ei, dr, di = r[:half, :frame], r[half:, :frame], r[:half, frame:], r[half:, frame:]
            vr, vi = dr * c + di * s, di * c - dr * s
            yr = cat([er + vr, er - vr], axis=0)
            yi = cat([ei + vi, ei - vi], axis=0)
            x = cat(
                [cat([yr[:, :half], yi[:, :half]], axis=1), cat([yr[:, half:], yi[:, half:]], axis=1)],
                axis=0,
            )
            y = right_dot(x, ri[...])
            c, s = twr[0, 0:1], twr[1, 0:1]
            er, ei, dr, di = y[:frame, :half], y[:frame, half:], y[frame:, :half], y[frame:, half:]
            vr, vi = dr * c + di * s, di * c - dr * s
            qr, qi, pr, pi = accum[0], accum[1], probe[0, m], probe[1, m]
            br = (cat([er + vr, er - vr], axis=1) - (pr * qr - pi * qi)) * flag
            bi = (cat([ei + vi, ei - vi], axis=1) - (pr * qi + pi * qr)) * flag
            accum[2] += pr * br + pi * bi
            accum[3] += pr * bi - pi * br
            accum[4] += flag * (pr * pr + pi * pi)
            gr, gi = qr * br + qi * bi, qr * bi - qi * br
            if slot == 0:
                grad[0, m], grad[1, m] = gr, gi
            else:
                grad[0, m] += gr
                grad[1, m] += gi

        strength = flag * (qr * qr + qi * qi)
        power[...] = strength if slot == 0 else power[...] + strength
        for part in range(3):
            piece = accum[2 + part]
            piece = cat([piece, jnp.zeros((frame, width - frame), F32)], axis=1)
            piece = pltpu.roll(piece, col, 1)
            piece = cat([piece, jnp.zeros((height - frame, width), F32)], axis=0)
            piece = pltpu.roll(piece, row, 0)
            totals[part] = piece if slot == 0 else totals[part] + piece


def waves(place, live, own, right, down, diag, probe, amplitude):
    modes, frame = probe.shape[1], probe.shape[2]
    tile = own.shape[1]
    smem = pl.BlockSpec(memory_space=pltpu.SMEM)
    vmem = pl.BlockSpec(memory_space=pltpu.VMEM)
    return pl.pallas_call(
        waves_kernel,
        out_shape=(
            jax.ShapeDtypeStruct((3, 2 * tile, 2 * tile), F32),
            jax.ShapeDtypeStruct(probe.shape, F32),
            jax.ShapeDtypeStruct((frame, frame), F32),
        ),
        in_specs=[smem] * 2 + [vmem] * 12,
        out_specs=(vmem, vmem, vmem),
        scratch_shapes=[
            pltpu.VMEM((modes, frame, 2 * frame), F32),
            pltpu.VMEM((frame, 2 * frame), F32),
            pltpu.VMEM((5, frame, frame), F32),
        ],
        compiler_params=pltpu.CompilerParams(vmem_limit_bytes=48 << 20),
        cost_estimate=pl.CostEstimate(
            flops=60_000_000_000, bytes_accessed=16 << 20, transcendentals=0
        ),
    )(place, live, own, right, down, diag, probe, amplitude, *tables(frame))


def moved(value, down, right):
    rows, cols = lax.axis_size("row"), lax.axis_size("col")
    pairs = [
        (r * cols + c, (r + down) * cols + c + right)
        for r in range(rows)
        for c in range(cols)
        if 0 <= r + down < rows and 0 <= c + right < cols
    ]
    return lax.ppermute(value, ("row", "col"), pairs)


def per_device(object_field, probe_modes, patterns, offsets, counts):
    tile, frame = object_field.shape[1], probe_modes.shape[-1]
    slots = patterns.shape[0]
    right = moved(object_field, 0, -1)
    down = moved(object_field, -1, 0)
    diag = moved(object_field, -1, -1)
    base = jnp.stack([lax.axis_index("row"), lax.axis_index("col")]).astype(jnp.int32) * tile
    place = offsets - base[:, None]
    live = (jnp.arange(slots, dtype=jnp.int32) < counts[0]).astype(jnp.int32)
    half = frame // 2
    amplitude = patterns.reshape(slots, half, 2, half, 2).transpose(0, 2, 1, 4, 3)
    amplitude = amplitude.reshape(slots, frame, frame)
    totals, gradient, power = waves(
        place, live, object_field, right, down, diag, probe_modes, amplitude
    )
    gradient_all, power_all = lax.psum((gradient, power), ("row", "col"))
    sums = totals[:, :tile, :tile] + moved(totals[:, :tile, tile:], 0, 1)
    sums = sums + moved(totals[:, tile:, :tile], 1, 0) + moved(totals[:, tile:, tile:], 1, 1)
    updated = object_field + sums[:2] / (sums[2] + OBJECT_DELTA)
    above = moved(updated[:, -1, :], 1, 0)
    below = moved(updated[:, 0, :], -1, 0)
    before = moved(updated[:, :, -1], 0, 1)
    after = moved(updated[:, :, 0], 0, -1)
    neighbours = (
        jnp.concatenate([updated[:, 1:], below[:, None]], axis=1)
        + jnp.concatenate([above[:, None], updated[:, :-1]], axis=1)
        + jnp.concatenate([updated[:, :, 1:], after[:, :, None]], axis=2)
        + jnp.concatenate([before[:, :, None], updated[:, :, :-1]], axis=2)
    )
    new_object = updated + SMOOTH_WEIGHT * (neighbours - 4.0 * updated)
    new_probe = probe_modes + gradient_all / (power_all[None, None] + PROBE_DELTA)
    return (new_object, new_probe)


def solution(mesh):
    return jax.shard_map(
        per_device,
        mesh=mesh,
        in_specs=(
            P(None, "row", "col"),
            P(),
            P(("row", "col"), None, None),
            P(None, ("row", "col")),
            P(("row", "col")),
        ),
        out_specs=(P(None, "row", "col"), P()),
        check_vma=False,
    )
```

```python
import functools
import math

import jax
import jax.numpy as jnp
import ml_dtypes
import numpy as np
from jax import lax
from jax.experimental import pallas as pl
from jax.experimental.pallas import tpu as pltpu
from jax.sharding import PartitionSpec as P

INTENSITY_FLOOR = 0.1
OBJECT_DELTA = 0.5
PROBE_DELTA = 1.0
SMOOTH_WEIGHT = 0.1
F32 = jnp.float32
BF16 = jnp.bfloat16


def tables(frame):
    half = frame // 2
    n = np.arange(half)
    angle = -2.0 * np.pi * (np.outer(n, n) % half) / half
    c, s = np.cos(angle) / math.sqrt(frame), np.sin(angle) / math.sqrt(frame)
    full = np.block([[c, s], [-s, c]]).astype(np.float32)
    high = full.astype(ml_dtypes.bfloat16)
    low = (full - high.astype(np.float32)).astype(ml_dtypes.bfloat16)
    right_f = np.concatenate([high, high, low], axis=0)
    right_i = np.concatenate([high.T, high.T, low.T], axis=0)
    left_f = np.concatenate([high.T, high.T, low.T], axis=1)
    left_i = np.concatenate([high, high, low], axis=1)
    turn = -2.0 * np.pi * n / frame
    tw = np.stack([np.cos(turn), np.sin(turn)]).astype(np.float32)
    rows = np.broadcast_to(tw[:, None, :], (2, 8, half)).copy()
    cols = np.broadcast_to(tw[:, :, None], (2, half, frame)).copy()
    order = np.arange(frame)
    order = np.where(order < half, 2 * order, 2 * (order - half) + 1)
    move = np.eye(frame)[order].astype(ml_dtypes.bfloat16)
    moves = np.concatenate([move, move, move], axis=1)
    return right_f, right_i, left_f, left_i, rows, cols, moves, moves.T.copy()


def split(x):
    high = x.astype(BF16)
    return high, (x - high.astype(F32)).astype(BF16)


def split_exact(x):
    high = x.astype(BF16)
    rest = x - high.astype(F32)
    return (high,) + split(rest)


def right_dot(x, table):
    high, low = split(x)
    return jnp.dot(jnp.concatenate([high, low, high], axis=1), table, preferred_element_type=F32)


def left_dot(table, x):
    high, low = split(x)
    return jnp.dot(table, jnp.concatenate([high, low, high], axis=0), preferred_element_type=F32)


def waves_kernel(
    place, live, own, right, down, diag, probe, amplitude, rf, ri, lf, li, twr, twc, rows_to, cols_to,
    totals, grad, spectra, ratio, accum,
):
    modes, frame = probe.shape[1], probe.shape[2]
    half = frame // 2
    slots = amplitude.shape[0]
    tile = own.shape[1]
    cat = jnp.concatenate

    def put(plane, value, first):
        blocks = frame // 8
        for part in range(frame // 128):
            where = pl.ds((plane * (frame // 128) + part) * blocks, blocks)
            piece = value[:, part * 128 : (part + 1) * 128].reshape(blocks, 8, 128)
            grad[where] = piece if first else grad[where] + piece

    used = (2 * modes + 1) * (frame // 128) * (frame // 8)
    if grad.shape[0] > used:
        grad[used:] = jnp.zeros((grad.shape[0] - used, 8, 128), F32)

    for slot in range(slots):
        row, col = place[0, slot], place[1, slot]
        flag = live[slot].astype(F32)
        height, width = 2 * tile, 2 * tile
        patch = []
        for part in range(2):
            whole = cat(
                [cat([own[part], right[part]], axis=1), cat([down[part], diag[part]], axis=1)], axis=0
            )
            whole = pltpu.roll(whole, lax.rem(height - row, height), 0)[:frame]
            patch.append(pltpu.roll(whole, lax.rem(width - col, width), 1)[:, :frame])
        qr, qi = patch
        accum[0], accum[1] = qr, qi
        accum[2] = jnp.zeros((frame, frame), F32)

        @pl.loop(0, modes)
        def _(m):
            qr, qi, pr, pi = accum[0], accum[1], probe[0, m], probe[1, m]
            wr, wi = pr * qr - pi * qi, pr * qi + pi * qr
            c, s = twr[0, 0:1], twr[1, 0:1]
            dr, di = wr[:, :half] - wr[:, half:], wi[:, :half] - wi[:, half:]
            x = cat(
                [
                    cat([wr[:, :half] + wr[:, half:], wi[:, :half] + wi[:, half:]], axis=1),
                    cat([dr * c - di * s, dr * s + di * c], axis=1),
                ],
                axis=0,
            )
            y = right_dot(x, rf[...])
            yr = cat([y[:frame, :half], y[frame:, :half]], axis=1)
            yi = cat([y[:frame, half:], y[frame:, half:]], axis=1)
            c, s = twc[0], twc[1]
            dr, di = yr[:half] - yr[half:], yi[:half] - yi[half:]
            z = cat(
                [
                    cat([yr[:half] + yr[half:], yi[:half] + yi[half:]], axis=0),
                    cat([dr * c - di * s, dr * s + di * c], axis=0),
                ],
                axis=1,
            )
            r = left_dot(lf[...], z)
            spectra[m] = r
            accum[2] += cat(
                [
                    r[:half, :frame] * r[:half, :frame] + r[half:, :frame] * r[half:, :frame],
                    r[:half, frame:] * r[:half, frame:] + r[half:, frame:] * r[half:, frame:],
                ],
                axis=0,
            )

        sorted_cols = jnp.dot(
            cat(split_exact(amplitude[slot]), axis=1), cols_to[...], preferred_element_type=F32
        )
        sorted_all = jnp.dot(
            rows_to[...], cat(split_exact(sorted_cols), axis=0), preferred_element_type=F32
        )
        scale = sorted_all * lax.rsqrt(jnp.maximum(accum[2], INTENSITY_FLOOR))
        ratio[:half, :frame] = scale[:half]
        ratio[half:, :frame] = scale[:half]
        ratio[:half, frame:] = scale[half:]
        ratio[half:, frame:] = scale[half:]
        for part in range(3):
            accum[2 + part] = jnp.zeros((frame, frame), F32)

        @pl.loop(0, modes)
        def _(m):
            r = left_dot(li[...], spectra[m] * ratio[...])
            c, s = twc[0], twc[1]
            er, ei, dr, di = r[:half, :frame], r[half:, :frame], r[:half, frame:], r[half:, frame:]
            vr, vi = dr * c + di * s, di * c - dr * s
            yr = cat([er + vr, er - vr], axis=0)
            yi = cat([ei + vi, ei - vi], axis=0)
            x = cat(
                [cat([yr[:, :half], yi[:, :half]], axis=1), cat([yr[:, half:], yi[:, half:]], axis=1)],
                axis=0,
            )
            y = right_dot(x, ri[...])
            c, s = twr[0, 0:1], twr[1, 0:1]
            er, ei, dr, di = y[:frame, :half], y[:frame, half:], y[frame:, :half], y[frame:, half:]
            vr, vi = dr * c + di * s, di * c - dr * s
            qr, qi, pr, pi = accum[0], accum[1], probe[0, m], probe[1, m]
            br = (cat([er + vr, er - vr], axis=1) - (pr * qr - pi * qi)) * flag
            bi = (cat([ei + vi, ei - vi], axis=1) - (pr * qi + pi * qr)) * flag
            accum[2] += pr * br + pi * bi
            accum[3] += pr * bi - pi * br
            accum[4] += flag * (pr * pr + pi * pi)
            gr, gi = qr * br + qi * bi, qr * bi - qi * br
            put(m, gr, slot == 0)
            put(modes + m, gi, slot == 0)

        strength = flag * (qr * qr + qi * qi)
        put(2 * modes, strength, slot == 0)
        for part in range(3):
            piece = accum[2 + part]
            piece = cat([piece, jnp.zeros((frame, width - frame), F32)], axis=1)
            piece = pltpu.roll(piece, col, 1)
            piece = cat([piece, jnp.zeros((height - frame, width), F32)], axis=0)
            piece = pltpu.roll(piece, row, 0)
            totals[part] = piece if slot == 0 else totals[part] + piece


def waves(place, live, own, right, down, diag, probe, amplitude, chunks):
    modes, frame = probe.shape[1], probe.shape[2]
    tile = own.shape[1]
    smem = pl.BlockSpec(memory_space=pltpu.SMEM)
    vmem = pl.BlockSpec(memory_space=pltpu.VMEM)
    return pl.pallas_call(
        waves_kernel,
        out_shape=(
            jax.ShapeDtypeStruct((3, 2 * tile, 2 * tile), F32),
            jax.ShapeDtypeStruct((chunks, 8, 128), F32),
        ),
        in_specs=[smem] * 2 + [vmem] * 14,
        out_specs=(vmem, vmem),
        scratch_shapes=[
            pltpu.VMEM((modes, frame, 2 * frame), F32),
            pltpu.VMEM((frame, 2 * frame), F32),
            pltpu.VMEM((5, frame, frame), F32),
        ],
        compiler_params=pltpu.CompilerParams(vmem_limit_bytes=48 << 20),
        cost_estimate=pl.CostEstimate(
            flops=60_000_000_000, bytes_accessed=16 << 20, transcendentals=0
        ),
    )(place, live, own, right, down, diag, probe, amplitude, *tables(frame))


def moved(value, down, right):
    rows, cols = lax.axis_size("row"), lax.axis_size("col")
    pairs = [
        (r * cols + c, (r + down) * cols + c + right)
        for r in range(rows)
        for c in range(cols)
        if 0 <= r + down < rows and 0 <= c + right < cols
    ]
    return lax.ppermute(value, ("row", "col"), pairs)


def exchange_kernel(
    rows, cols, parts, grad, totals, own, probe, new_object, new_probe,
    acc, inbox, full, quads, upd, row_edges, col_edges, inverse,
    send_sem, recv_sem, quad_send, quad_recv, edge_send, edge_recv,
):
    r, c = lax.axis_index("row"), lax.axis_index("col")
    tile = own.shape[1]
    modes, frame = probe.shape[1], probe.shape[2]
    row_bits, col_bits = rows.bit_length() - 1, cols.bit_length() - 1
    core = [(0, bit) for bit in range(row_bits)][:1]
    far = [(0, bit) for bit in range(row_bits)][1:]
    low = [(1, bit) for bit in range(col_bits // 2)]
    high = [(1, bit) for bit in range(col_bits // 2, col_bits)]
    orders = [core + far + low + high, core + low + high + far, core + high + far + low]
    stages = row_bits + col_bits

    def partner(axis, bit):
        step = 1 << bit
        mine = (c if axis else r) // step % 2
        shift = step - 2 * step * mine
        return mine, ((r, c + shift) if axis else (r + shift, c))

    def near(dr, dc):
        good = jnp.bool_(True)
        if dr > 0:
            good = jnp.logical_and(good, r < rows - dr)
        if dr < 0:
            good = jnp.logical_and(good, r >= -dr)
        if dc > 0:
            good = jnp.logical_and(good, c < cols - dc)
        if dc < 0:
            good = jnp.logical_and(good, c >= -dc)
        return good, (r + dr, c + dc)

    row_edges[...] = jnp.zeros_like(row_edges)
    col_edges[...] = jnp.zeros_like(col_edges)
    barrier = pltpu.get_barrier_semaphore()
    for axis, bit in orders[0]:
        pl.semaphore_signal(
            barrier, inc=1, device_id=partner(axis, bit)[1], device_id_type=pl.DeviceIdType.MESH
        )
    expected = jnp.int32(stages)
    for dr, dc in ((0, 1), (1, 0), (1, 1), (0, -1), (-1, 0), (-1, -1)):
        good, there = near(dr, dc)

        @pl.when(good)
        def _():
            pl.semaphore_signal(
                barrier, inc=1, device_id=there, device_id_type=pl.DeviceIdType.MESH
            )

        expected = expected + jnp.where(good, 1, 0)
    pl.semaphore_wait(barrier, expected)

    def remote(source, target, send, recv, there):
        return pltpu.make_async_remote_copy(
            src_ref=source, dst_ref=target, send_sem=send, recv_sem=recv,
            device_id=there, device_id_type=pl.DeviceIdType.MESH,
        )

    ranges = [[start] for start in parts]
    slots = [0]
    copies = {}

    def halve(p, stage):
        start, size = ranges[p][stage]
        mine, there = partner(*orders[p][stage])
        half = size // 2
        box = pl.ds(slots[0], half)
        slots[0] += half
        source = (grad if stage == 0 else acc).at[pl.ds(start + (1 - mine) * half, half)]
        copy = remote(
            source, inbox.at[box], send_sem.at[0, p, stage], recv_sem.at[0, p, stage], there
        )
        copy.start()
        ranges[p].append((start + mine * half, half))
        copies[p, stage] = (copy, box)

    def add(p, stage):
        copy, box = copies[p, stage]
        copy.wait()
        keep = pl.ds(*ranges[p][stage + 1])
        target = full if stage + 1 == stages else acc
        target[keep] = (grad if stage == 0 else acc)[keep] + inbox[box]

    def spread(p, stage):
        there = partner(*orders[p][stage])[1]
        keep = pl.ds(*ranges[p][stage + 1])
        copy = remote(
            full.at[keep], full.at[keep], send_sem.at[1, p, stage], recv_sem.at[1, p, stage], there
        )
        copy.start()
        copies[p, stage] = (copy, None)

    every = range(len(parts))
    for p in every:
        halve(p, 0)
    sides = ((0, 1), (1, 0), (1, 1))
    quadrants = []
    for k, (dr, dc) in enumerate(sides):
        source = totals.at[:, pl.ds(dr * tile, tile), pl.ds(dc * tile, tile)]
        good, there = near(dr, dc)
        copy = remote(source, quads.at[k], quad_send.at[k], quad_recv.at[k], there)
        pl.when(good)(copy.start)
        quadrants.append((good, near(-dr, -dc)[0], copy))
    for stage in range(stages):
        for p in every:
            add(p, stage)
            if stage + 1 < stages:
                halve(p, stage + 1)
            else:
                spread(p, stage)

    def update():
        upd[...] = totals[:, :tile, :tile]
        for k, (good, gets, copy) in enumerate(quadrants):
            pl.when(good)(copy.wait_send)

            @pl.when(gets)
            def _():
                copy.wait_recv()
                upd[...] += quads[k]

        below = upd[2] + OBJECT_DELTA
        upd[0] = own[0] + upd[0] / below
        upd[1] = own[1] + upd[1] / below
        borders = (
            ((1, 0), upd.at[:2, pl.ds(tile - 8, 8)], row_edges.at[0]),
            ((-1, 0), upd.at[:2, pl.ds(0, 8)], row_edges.at[1]),
            ((0, 1), upd.at[:2, :, pl.ds(tile - 128, 128)], col_edges.at[0]),
            ((0, -1), upd.at[:2, :, pl.ds(0, 128)], col_edges.at[1]),
        )
        edges = []
        for k, ((dr, dc), source, target) in enumerate(borders):
            good, there = near(dr, dc)
            copy = remote(source, target, edge_send.at[k], edge_recv.at[k], there)
            pl.when(good)(copy.start)
            edges.append((good, near(-dr, -dc)[0], copy))
        return edges

    def smooth(edges):
        for good, gets, copy in edges:
            pl.when(good)(copy.wait_send)
            pl.when(gets)(copy.wait_recv)
        for part in range(2):
            value = upd[part]
            above, below = row_edges[0, part, 7:8], row_edges[1, part, 0:1]
            before, after = col_edges[0, part][:, 127:128], col_edges[1, part][:, 0:1]
            neighbours = (
                jnp.concatenate([value[1:], below], axis=0)
                + jnp.concatenate([above, value[:-1]], axis=0)
                + jnp.concatenate([value[:, 1:], after], axis=1)
                + jnp.concatenate([before, value[:, :-1]], axis=1)
            )
            new_object[part] = value + SMOOTH_WEIGHT * (neighbours - 4.0 * value)

    update_at, smooth_at = min(2, stages - 1), min(1, stages - 1)
    edges = None
    for stage in reversed(range(stages)):
        for p in every:
            copies[p, stage][0].wait()
            if stage > 0:
                spread(p, stage - 1)
        if stage == update_at:
            edges = update()
        if stage == smooth_at:
            smooth(edges)

    blocks = frame // 8
    for part in range(frame // 128):
        lanes = pl.ds(part * 128, 128)

        def plane(index):
            where = pl.ds((index * (frame // 128) + part) * blocks, blocks)
            return full[where].reshape(frame, 128)

        inverse[...] = 1.0 / (plane(2 * modes) + PROBE_DELTA)

        @pl.loop(0, modes)
        def _(m):
            new_probe[0, m, :, lanes] = probe[0, m, :, lanes] + plane(m) * inverse[...]
            new_probe[1, m, :, lanes] = probe[1, m, :, lanes] + plane(modes + m) * inverse[...]


def cut(probe, devices):
    modes, frame = probe.shape[1], probe.shape[2]
    used = (2 * modes + 1) * (frame // 128) * (frame // 8)
    units = -(-used // devices)
    bounds = [units * k // 3 * devices for k in range(4)]
    return units * devices, [(a, b - a) for a, b in zip(bounds, bounds[1:]) if b > a]


def exchange(grad, totals, own, probe, parts):
    rows, cols = lax.axis_size("row"), lax.axis_size("col")
    frame, tile = probe.shape[2], own.shape[1]
    stages = (rows * cols).bit_length() - 1
    vmem = pl.BlockSpec(memory_space=pltpu.VMEM)
    dma = pltpu.SemaphoreType.DMA
    return pl.pallas_call(
        functools.partial(exchange_kernel, rows, cols, parts),
        out_shape=(
            jax.ShapeDtypeStruct(own.shape, F32),
            jax.ShapeDtypeStruct(probe.shape, F32),
        ),
        in_specs=[vmem] * 4,
        out_specs=(vmem, vmem),
        scratch_shapes=[
            pltpu.VMEM(grad.shape, F32),
            pltpu.VMEM(grad.shape, F32),
            pltpu.VMEM(grad.shape, F32),
            pltpu.VMEM((3, 3, tile, tile), F32),
            pltpu.VMEM((3, tile, tile), F32),
            pltpu.VMEM((2, 2, 8, tile), F32),
            pltpu.VMEM((2, 2, tile, 128), F32),
            pltpu.VMEM((frame, 128), F32),
            dma((2, len(parts), stages)),
            dma((2, len(parts), stages)),
            dma((3,)),
            dma((3,)),
            dma((4,)),
            dma((4,)),
        ],
        compiler_params=pltpu.CompilerParams(
            vmem_limit_bytes=48 << 20, collective_id=0, has_side_effects=True
        ),
        cost_estimate=pl.CostEstimate(flops=1 << 22, bytes_accessed=24 << 20, transcendentals=0),
    )(grad, totals, own, probe)


def per_device(object_field, probe_modes, patterns, offsets, counts):
    tile, frame = object_field.shape[1], probe_modes.shape[-1]
    slots = patterns.shape[0]
    right = moved(object_field, 0, -1)
    down = moved(object_field, -1, 0)
    diag = moved(object_field, -1, -1)
    base = jnp.stack([lax.axis_index("row"), lax.axis_index("col")]).astype(jnp.int32) * tile
    place = offsets - base[:, None]
    live = (jnp.arange(slots, dtype=jnp.int32) < counts[0]).astype(jnp.int32)
    chunks, parts = cut(probe_modes, lax.axis_size("row") * lax.axis_size("col"))
    totals, gradient = waves(
        place, live, object_field, right, down, diag, probe_modes, patterns, chunks
    )
    return exchange(gradient, totals, object_field, probe_modes, parts)


def solution(mesh):
    return jax.shard_map(
        per_device,
        mesh=mesh,
        in_specs=(
            P(None, "row", "col"),
            P(),
            P(("row", "col"), None, None),
            P(None, ("row", "col")),
            P(("row", "col")),
        ),
        out_specs=(P(None, "row", "col"), P()),
        check_vma=False,
    )
```

```python
import functools
import math

import jax
import jax.numpy as jnp
import ml_dtypes
import numpy as np
from jax import lax
from jax.experimental import pallas as pl
from jax.experimental.pallas import tpu as pltpu
from jax.sharding import PartitionSpec as P

INTENSITY_FLOOR = 0.1
OBJECT_DELTA = 0.5
PROBE_DELTA = 1.0
SMOOTH_WEIGHT = 0.1
F32 = jnp.float32
BF16 = jnp.bfloat16
UNROLL = 1


def tables(frame):
    half = frame // 2
    n = np.arange(half)
    angle = -2.0 * np.pi * (np.outer(n, n) % half) / half
    c, s = np.cos(angle) / math.sqrt(frame), np.sin(angle) / math.sqrt(frame)
    full = np.block([[c, s], [-s, c]]).astype(np.float32)
    high = full.astype(ml_dtypes.bfloat16)
    low = (full - high.astype(np.float32)).astype(ml_dtypes.bfloat16)
    turn = -2.0 * np.pi * n / frame
    tw = np.stack([np.cos(turn), np.sin(turn)]).astype(np.float32)
    rows = np.zeros((2, 8, frame), np.float32)
    rows[:, :, :half] = tw[:, None, :]
    cols = np.broadcast_to(tw[:, :, None], (2, half, frame))
    order = np.arange(frame)
    order = np.where(order < half, 2 * order, 2 * (order - half) + 1)
    move = np.eye(frame)[order].astype(ml_dtypes.bfloat16)
    return np.stack([high, low, high.T, low.T, move, move.T]), np.concatenate([cols, rows], axis=1)


def split(x):
    high = x.astype(BF16)
    return high, (x - high.astype(F32)).astype(BF16)


def split_exact(x):
    high = x.astype(BF16)
    rest = x - high.astype(F32)
    return (high,) + split(rest)


def right_dot(x, table):
    high, low = split(x)
    return jnp.dot(jnp.concatenate([high, low, high], axis=1), table, preferred_element_type=F32)


def left_dot(table, x):
    high, low = split(x)
    return jnp.dot(table, jnp.concatenate([high, low, high], axis=0), preferred_element_type=F32)


def waves_kernel(
    place, live, own, right, down, diag, probe, amplitude, matrices, turns,
    totals, grad, spectra, ratio, accum,
):
    modes, frame = probe.shape[1], probe.shape[2]
    half = frame // 2
    slots = amplitude.shape[0]
    tile = own.shape[1]
    cat = jnp.concatenate

    def stacked(high, low, axis):
        return cat([matrices[high], matrices[high], matrices[low]], axis=axis)

    def put(plane, value, first):
        blocks = frame // 8
        for part in range(frame // 128):
            where = pl.ds((plane * (frame // 128) + part) * blocks, blocks)
            piece = value[:, part * 128 : (part + 1) * 128].reshape(blocks, 8, 128)
            grad[where] = piece if first else grad[where] + piece

    used = (2 * modes + 1) * (frame // 128) * (frame // 8)
    if grad.shape[0] > used:
        grad[used:] = jnp.zeros((grad.shape[0] - used, 8, 128), F32)

    for slot in range(slots):
        row, col = place[0, slot], place[1, slot]
        flag = live[slot].astype(F32)
        height, width = 2 * tile, 2 * tile
        patch = []
        for part in range(2):
            whole = cat(
                [cat([own[part], right[part]], axis=1), cat([down[part], diag[part]], axis=1)], axis=0
            )
            whole = pltpu.roll(whole, lax.rem(height - row, height), 0)[:frame]
            patch.append(pltpu.roll(whole, lax.rem(width - col, width), 1)[:, :frame])
        qr, qi = patch
        accum[0], accum[1] = qr, qi
        accum[2] = jnp.zeros((frame, frame), F32)

        @pl.loop(0, modes, unroll=UNROLL)
        def _(m):
            qr, qi, pr, pi = accum[0], accum[1], probe[0, m], probe[1, m]
            wr, wi = pr * qr - pi * qi, pr * qi + pi * qr
            c, s = turns[0, half : half + 1, :half], turns[1, half : half + 1, :half]
            dr, di = wr[:, :half] - wr[:, half:], wi[:, :half] - wi[:, half:]
            x = cat(
                [
                    cat([wr[:, :half] + wr[:, half:], wi[:, :half] + wi[:, half:]], axis=1),
                    cat([dr * c - di * s, dr * s + di * c], axis=1),
                ],
                axis=0,
            )
            y = right_dot(x, stacked(0, 1, 0))
            yr = cat([y[:frame, :half], y[frame:, :half]], axis=1)
            yi = cat([y[:frame, half:], y[frame:, half:]], axis=1)
            c, s = turns[0, :half], turns[1, :half]
            dr, di = yr[:half] - yr[half:], yi[:half] - yi[half:]
            z = cat(
                [
                    cat([yr[:half] + yr[half:], yi[:half] + yi[half:]], axis=0),
                    cat([dr * c - di * s, dr * s + di * c], axis=0),
                ],
                axis=1,
            )
            r = left_dot(stacked(2, 3, 1), z)
            spectra[m] = r
            accum[2] += cat(
                [
                    r[:half, :frame] * r[:half, :frame] + r[half:, :frame] * r[half:, :frame],
                    r[:half, frame:] * r[:half, frame:] + r[half:, frame:] * r[half:, frame:],
                ],
                axis=0,
            )

        sorted_cols = jnp.dot(
            cat(split_exact(amplitude[slot]), axis=1), stacked(5, 5, 0), preferred_element_type=F32
        )
        sorted_all = jnp.dot(
            stacked(4, 4, 1), cat(split_exact(sorted_cols), axis=0), preferred_element_type=F32
        )
        scale = sorted_all * lax.rsqrt(jnp.maximum(accum[2], INTENSITY_FLOOR))
        ratio[:half, :frame] = scale[:half]
        ratio[half:, :frame] = scale[:half]
        ratio[:half, frame:] = scale[half:]
        ratio[half:, frame:] = scale[half:]
        for part in range(3):
            accum[2 + part] = jnp.zeros((frame, frame), F32)

        @pl.loop(0, modes, unroll=UNROLL)
        def _(m):
            r = left_dot(stacked(0, 1, 1), spectra[m] * ratio[...])
            c, s = turns[0, :half], turns[1, :half]
            er, ei, dr, di = r[:half, :frame], r[half:, :frame], r[:half, frame:], r[half:, frame:]
            vr, vi = dr * c + di * s, di * c - dr * s
            yr = cat([er + vr, er - vr], axis=0)
            yi = cat([ei + vi, ei - vi], axis=0)
            x = cat(
                [cat([yr[:, :half], yi[:, :half]], axis=1), cat([yr[:, half:], yi[:, half:]], axis=1)],
                axis=0,
            )
            y = right_dot(x, stacked(2, 3, 0))
            c, s = turns[0, half : half + 1, :half], turns[1, half : half + 1, :half]
            er, ei, dr, di = y[:frame, :half], y[:frame, half:], y[frame:, :half], y[frame:, half:]
            vr, vi = dr * c + di * s, di * c - dr * s
            qr, qi, pr, pi = accum[0], accum[1], probe[0, m], probe[1, m]
            br = (cat([er + vr, er - vr], axis=1) - (pr * qr - pi * qi)) * flag
            bi = (cat([ei + vi, ei - vi], axis=1) - (pr * qi + pi * qr)) * flag
            accum[2] += pr * br + pi * bi
            accum[3] += pr * bi - pi * br
            accum[4] += flag * (pr * pr + pi * pi)
            gr, gi = qr * br + qi * bi, qr * bi - qi * br
            put(m, gr, slot == 0)
            put(modes + m, gi, slot == 0)

        strength = flag * (qr * qr + qi * qi)
        put(2 * modes, strength, slot == 0)
        for part in range(3):
            piece = accum[2 + part]
            piece = cat([piece, jnp.zeros((frame, width - frame), F32)], axis=1)
            piece = pltpu.roll(piece, col, 1)
            piece = cat([piece, jnp.zeros((height - frame, width), F32)], axis=0)
            piece = pltpu.roll(piece, row, 0)
            totals[part] = piece if slot == 0 else totals[part] + piece


def waves(place, live, own, right, down, diag, probe, amplitude, chunks):
    modes, frame = probe.shape[1], probe.shape[2]
    tile = own.shape[1]
    smem = pl.BlockSpec(memory_space=pltpu.SMEM)
    vmem = pl.BlockSpec(memory_space=pltpu.VMEM)
    return pl.pallas_call(
        waves_kernel,
        out_shape=(
            jax.ShapeDtypeStruct((3, 2 * tile, 2 * tile), F32),
            jax.ShapeDtypeStruct((chunks, 8, 128), F32),
        ),
        in_specs=[smem] * 2 + [vmem] * 8,
        out_specs=(vmem, vmem),
        scratch_shapes=[
            pltpu.VMEM((modes, frame, 2 * frame), F32),
            pltpu.VMEM((frame, 2 * frame), F32),
            pltpu.VMEM((5, frame, frame), F32),
        ],
        compiler_params=pltpu.CompilerParams(vmem_limit_bytes=48 << 20),
        cost_estimate=pl.CostEstimate(
            flops=60_000_000_000, bytes_accessed=16 << 20, transcendentals=0
        ),
    )(place, live, own, right, down, diag, probe, amplitude, *tables(frame))


def moved(value, down, right):
    rows, cols = lax.axis_size("row"), lax.axis_size("col")
    pairs = [
        (r * cols + c, (r + down) * cols + c + right)
        for r in range(rows)
        for c in range(cols)
        if 0 <= r + down < rows and 0 <= c + right < cols
    ]
    return lax.ppermute(value, ("row", "col"), pairs)


def exchange_kernel(
    rows, cols, parts, grad, totals, own, probe, new_object, new_probe,
    acc, inbox, full, fallen, wide, pushed, upd, row_edges, col_edges, inverse,
    send_sem, recv_sem, quad_send, quad_recv, edge_send, edge_recv,
):
    r, c = lax.axis_index("row"), lax.axis_index("col")
    tile = own.shape[1]
    modes, frame = probe.shape[1], probe.shape[2]
    row_bits, col_bits = rows.bit_length() - 1, cols.bit_length() - 1
    core = [(0, bit) for bit in range(row_bits)][:1]
    far = [(0, bit) for bit in range(row_bits)][1:]
    low = [(1, bit) for bit in range(col_bits // 2)]
    high = [(1, bit) for bit in range(col_bits // 2, col_bits)]
    orders = [core + far + low + high, core + low + high + far, core + high + far + low]
    stages = row_bits + col_bits

    def partner(axis, bit):
        step = 1 << bit
        mine = (c if axis else r) // step % 2
        shift = step - 2 * step * mine
        return mine, ((r, c + shift) if axis else (r + shift, c))

    def near(dr, dc):
        good = jnp.bool_(True)
        if dr > 0:
            good = jnp.logical_and(good, r < rows - dr)
        if dr < 0:
            good = jnp.logical_and(good, r >= -dr)
        if dc > 0:
            good = jnp.logical_and(good, c < cols - dc)
        if dc < 0:
            good = jnp.logical_and(good, c >= -dc)
        return good, (r + dr, c + dc)

    row_edges[...] = jnp.zeros_like(row_edges)
    col_edges[...] = jnp.zeros_like(col_edges)
    barrier = pltpu.get_barrier_semaphore()
    for axis, bit in orders[0]:
        pl.semaphore_signal(
            barrier, inc=1, device_id=partner(axis, bit)[1], device_id_type=pl.DeviceIdType.MESH
        )
    expected = jnp.int32(stages)
    for dr, dc in ((0, 1), (1, 0), (0, -1), (-1, 0)):
        good, there = near(dr, dc)

        @pl.when(good)
        def _():
            pl.semaphore_signal(
                barrier, inc=1, device_id=there, device_id_type=pl.DeviceIdType.MESH
            )

        expected = expected + jnp.where(good, 1, 0)
    pl.semaphore_wait(barrier, expected)

    def remote(source, target, send, recv, there):
        return pltpu.make_async_remote_copy(
            src_ref=source, dst_ref=target, send_sem=send, recv_sem=recv,
            device_id=there, device_id_type=pl.DeviceIdType.MESH,
        )

    ranges = [[start] for start in parts]
    slots = [0]
    copies = {}

    def halve(p, stage):
        start, size = ranges[p][stage]
        mine, there = partner(*orders[p][stage])
        half = size // 2
        box = pl.ds(slots[0], half)
        slots[0] += half
        source = (grad if stage == 0 else acc).at[pl.ds(start + (1 - mine) * half, half)]
        copy = remote(
            source, inbox.at[box], send_sem.at[0, p, stage], recv_sem.at[0, p, stage], there
        )
        copy.start()
        ranges[p].append((start + mine * half, half))
        copies[p, stage] = (copy, box)

    def add(p, stage):
        copy, box = copies[p, stage]
        copy.wait()
        keep = pl.ds(*ranges[p][stage + 1])
        target = full if stage + 1 == stages else acc
        target[keep] = (grad if stage == 0 else acc)[keep] + inbox[box]

    def spread(p, stage):
        there = partner(*orders[p][stage])[1]
        keep = pl.ds(*ranges[p][stage + 1])
        copy = remote(
            full.at[keep], full.at[keep], send_sem.at[1, p, stage], recv_sem.at[1, p, stage], there
        )
        copy.start()
        copies[p, stage] = (copy, None)

    every = range(len(parts))
    for p in every:
        halve(p, 0)
    def send_down():
        good, there = near(1, 0)
        copy = remote(
            totals.at[:, pl.ds(tile, tile)], fallen, quad_send.at[0], quad_recv.at[0], there
        )
        pl.when(good)(copy.start)
        return good, near(-1, 0)[0], copy

    def send_right(good, gets, copy):
        wide[...] = totals[:, :tile]
        pl.when(good)(copy.wait_send)

        @pl.when(gets)
        def _():
            copy.wait_recv()
            wide[...] += fallen[...]

        good, there = near(0, 1)
        copy = remote(
            wide.at[:, :, pl.ds(tile, tile)], pushed, quad_send.at[1], quad_recv.at[1], there
        )
        pl.when(good)(copy.start)
        return good, near(0, -1)[0], copy

    sideways = send_down()
    for stage in range(stages):
        for p in every:
            add(p, stage)
            if stage + 1 < stages:
                halve(p, stage + 1)
            else:
                spread(p, stage)
        if stage == min(1, stages - 1):
            sideways = send_right(*sideways)

    def update():
        good, gets, copy = sideways
        upd[...] = wide[:, :, :tile]
        pl.when(good)(copy.wait_send)

        @pl.when(gets)
        def _():
            copy.wait_recv()
            upd[...] += pushed[...]

        below = upd[2] + OBJECT_DELTA
        upd[0] = own[0] + upd[0] / below
        upd[1] = own[1] + upd[1] / below
        borders = (
            ((1, 0), upd.at[:2, pl.ds(tile - 8, 8)], row_edges.at[0]),
            ((-1, 0), upd.at[:2, pl.ds(0, 8)], row_edges.at[1]),
            ((0, 1), upd.at[:2, :, pl.ds(tile - 128, 128)], col_edges.at[0]),
            ((0, -1), upd.at[:2, :, pl.ds(0, 128)], col_edges.at[1]),
        )
        edges = []
        for k, ((dr, dc), source, target) in enumerate(borders):
            good, there = near(dr, dc)
            copy = remote(source, target, edge_send.at[k], edge_recv.at[k], there)
            pl.when(good)(copy.start)
            edges.append((good, near(-dr, -dc)[0], copy))
        return edges

    def smooth(edges):
        for good, gets, copy in edges:
            pl.when(good)(copy.wait_send)
            pl.when(gets)(copy.wait_recv)
        for part in range(2):
            value = upd[part]
            above, below = row_edges[0, part, 7:8], row_edges[1, part, 0:1]
            before, after = col_edges[0, part][:, 127:128], col_edges[1, part][:, 0:1]
            neighbours = (
                jnp.concatenate([value[1:], below], axis=0)
                + jnp.concatenate([above, value[:-1]], axis=0)
                + jnp.concatenate([value[:, 1:], after], axis=1)
                + jnp.concatenate([before, value[:, :-1]], axis=1)
            )
            new_object[part] = value + SMOOTH_WEIGHT * (neighbours - 4.0 * value)

    update_at, smooth_at = min(2, stages - 1), min(1, stages - 1)
    edges = None
    for stage in reversed(range(stages)):
        for p in every:
            copies[p, stage][0].wait()
            if stage > 0:
                spread(p, stage - 1)
        if stage == update_at:
            edges = update()
        if stage == smooth_at:
            smooth(edges)

    blocks = frame // 8
    for part in range(frame // 128):
        lanes = pl.ds(part * 128, 128)

        def plane(index):
            where = pl.ds((index * (frame // 128) + part) * blocks, blocks)
            return full[where].reshape(frame, 128)

        inverse[...] = 1.0 / (plane(2 * modes) + PROBE_DELTA)

        @pl.loop(0, modes)
        def _(m):
            new_probe[0, m, :, lanes] = probe[0, m, :, lanes] + plane(m) * inverse[...]
            new_probe[1, m, :, lanes] = probe[1, m, :, lanes] + plane(modes + m) * inverse[...]


def cut(probe, devices):
    modes, frame = probe.shape[1], probe.shape[2]
    used = (2 * modes + 1) * (frame // 128) * (frame // 8)
    units = -(-used // devices)
    bounds = [units * k // 3 * devices for k in range(4)]
    return units * devices, [(a, b - a) for a, b in zip(bounds, bounds[1:]) if b > a]


def exchange(grad, totals, own, probe, parts):
    rows, cols = lax.axis_size("row"), lax.axis_size("col")
    frame, tile = probe.shape[2], own.shape[1]
    stages = (rows * cols).bit_length() - 1
    vmem = pl.BlockSpec(memory_space=pltpu.VMEM)
    dma = pltpu.SemaphoreType.DMA
    return pl.pallas_call(
        functools.partial(exchange_kernel, rows, cols, parts),
        out_shape=(
            jax.ShapeDtypeStruct(own.shape, F32),
            jax.ShapeDtypeStruct(probe.shape, F32),
        ),
        in_specs=[vmem] * 4,
        out_specs=(vmem, vmem),
        scratch_shapes=[
            pltpu.VMEM(grad.shape, F32),
            pltpu.VMEM(grad.shape, F32),
            pltpu.VMEM(grad.shape, F32),
            pltpu.VMEM((3, tile, 2 * tile), F32),
            pltpu.VMEM((3, tile, 2 * tile), F32),
            pltpu.VMEM((3, tile, tile), F32),
            pltpu.VMEM((3, tile, tile), F32),
            pltpu.VMEM((2, 2, 8, tile), F32),
            pltpu.VMEM((2, 2, tile, 128), F32),
            pltpu.VMEM((frame, 128), F32),
            dma((2, len(parts), stages)),
            dma((2, len(parts), stages)),
            dma((2,)),
            dma((2,)),
            dma((4,)),
            dma((4,)),
        ],
        compiler_params=pltpu.CompilerParams(
            vmem_limit_bytes=48 << 20, collective_id=0, has_side_effects=True
        ),
        cost_estimate=pl.CostEstimate(flops=1 << 22, bytes_accessed=24 << 20, transcendentals=0),
    )(grad, totals, own, probe)


def per_device(object_field, probe_modes, patterns, offsets, counts):
    tile, frame = object_field.shape[1], probe_modes.shape[-1]
    slots = patterns.shape[0]
    right = moved(object_field, 0, -1)
    down = moved(object_field, -1, 0)
    diag = moved(object_field, -1, -1)
    base = jnp.stack([lax.axis_index("row"), lax.axis_index("col")]).astype(jnp.int32) * tile
    place = offsets - base[:, None]
    live = (jnp.arange(slots, dtype=jnp.int32) < counts[0]).astype(jnp.int32)
    chunks, parts = cut(probe_modes, lax.axis_size("row") * lax.axis_size("col"))
    totals, gradient = waves(
        place, live, object_field, right, down, diag, probe_modes, patterns, chunks
    )
    return exchange(gradient, totals, object_field, probe_modes, parts)


def solution(mesh):
    return jax.shard_map(
        per_device,
        mesh=mesh,
        in_specs=(
            P(None, "row", "col"),
            P(),
            P(("row", "col"), None, None),
            P(None, ("row", "col")),
            P(("row", "col")),
        ),
        out_specs=(P(None, "row", "col"), P()),
        check_vma=False,
    )
```

```python
import functools
import math

import jax
import jax.numpy as jnp
import ml_dtypes
import numpy as np
from jax import lax
from jax.experimental import pallas as pl
from jax.experimental.pallas import tpu as pltpu
from jax.sharding import PartitionSpec as P

INTENSITY_FLOOR = 0.1
OBJECT_DELTA = 0.5
PROBE_DELTA = 1.0
SMOOTH_WEIGHT = 0.1
F32 = jnp.float32
BF16 = jnp.bfloat16
UNROLL = 1


def tables(frame):
    half = frame // 2
    n = np.arange(half)
    angle = -2.0 * np.pi * (np.outer(n, n) % half) / half
    c, s = np.cos(angle) / math.sqrt(frame), np.sin(angle) / math.sqrt(frame)
    full = np.block([[c, s], [-s, c]]).astype(np.float32)
    high = full.astype(ml_dtypes.bfloat16)
    low = (full - high.astype(np.float32)).astype(ml_dtypes.bfloat16)
    turn = -2.0 * np.pi * n / frame
    tw = np.stack([np.cos(turn), np.sin(turn)]).astype(np.float32)
    rows = np.zeros((2, 8, frame), np.float32)
    rows[:, :, :half] = tw[:, None, :]
    cols = np.broadcast_to(tw[:, :, None], (2, half, frame))
    order = np.arange(frame)
    order = np.where(order < half, 2 * order, 2 * (order - half) + 1)
    move = np.eye(frame)[order].astype(ml_dtypes.bfloat16)
    return np.stack([high, low, high.T, low.T, move, move.T]), np.concatenate([cols, rows], axis=1)


def split(x):
    high = x.astype(BF16)
    return high, (x - high.astype(F32)).astype(BF16)


def split_exact(x):
    high = x.astype(BF16)
    rest = x - high.astype(F32)
    return (high,) + split(rest)


def right_dot(x, table):
    high, low = split(x)
    return jnp.dot(jnp.concatenate([high, low, high], axis=1), table, preferred_element_type=F32)


def left_dot(table, x):
    high, low = split(x)
    return jnp.dot(table, jnp.concatenate([high, low, high], axis=0), preferred_element_type=F32)


def waves_kernel(
    place, live, own, right, down, diag, probe, amplitude, matrices, turns,
    totals, grad, spectra, ratio, accum,
):
    modes, frame = probe.shape[1], probe.shape[2]
    half = frame // 2
    slots = amplitude.shape[0]
    tile = own.shape[1]
    cat = jnp.concatenate

    def stacked(high, low, axis):
        return cat([matrices[high], matrices[high], matrices[low]], axis=axis)

    def put(plane, value, first):
        blocks = frame // 8
        for part in range(frame // 128):
            where = pl.ds((plane * (frame // 128) + part) * blocks, blocks)
            piece = value[:, part * 128 : (part + 1) * 128].reshape(blocks, 8, 128)
            grad[where] = piece if first else grad[where] + piece

    used = (2 * modes + 1) * (frame // 128) * (frame // 8)
    if grad.shape[0] > used:
        grad[used:] = jnp.zeros((grad.shape[0] - used, 8, 128), F32)

    for slot in range(slots):
        row, col = place[0, slot], place[1, slot]
        flag = live[slot].astype(F32)
        height, width = 2 * tile, 2 * tile
        patch = []
        for part in range(2):
            whole = cat(
                [cat([own[part], right[part]], axis=1), cat([down[part], diag[part]], axis=1)], axis=0
            )
            whole = pltpu.roll(whole, lax.rem(height - row, height), 0)[:frame]
            patch.append(pltpu.roll(whole, lax.rem(width - col, width), 1)[:, :frame])
        qr, qi = patch
        accum[0], accum[1] = qr, qi
        accum[2] = jnp.zeros((frame, frame), F32)

        @pl.loop(0, modes, unroll=UNROLL)
        def _(m):
            qr, qi, pr, pi = accum[0], accum[1], probe[0, m], probe[1, m]
            wr, wi = pr * qr - pi * qi, pr * qi + pi * qr
            c, s = turns[0, half : half + 1, :half], turns[1, half : half + 1, :half]
            dr, di = wr[:, :half] - wr[:, half:], wi[:, :half] - wi[:, half:]
            x = cat(
                [
                    cat([wr[:, :half] + wr[:, half:], wi[:, :half] + wi[:, half:]], axis=1),
                    cat([dr * c - di * s, dr * s + di * c], axis=1),
                ],
                axis=0,
            )
            y = right_dot(x, stacked(0, 1, 0))
            yr = cat([y[:frame, :half], y[frame:, :half]], axis=1)
            yi = cat([y[:frame, half:], y[frame:, half:]], axis=1)
            c, s = turns[0, :half], turns[1, :half]
            dr, di = yr[:half] - yr[half:], yi[:half] - yi[half:]
            z = cat(
                [
                    cat([yr[:half] + yr[half:], yi[:half] + yi[half:]], axis=0),
                    cat([dr * c - di * s, dr * s + di * c], axis=0),
                ],
                axis=1,
            )
            r = left_dot(stacked(2, 3, 1), z)
            spectra[m] = r
            accum[2] += cat(
                [
                    r[:half, :frame] * r[:half, :frame] + r[half:, :frame] * r[half:, :frame],
                    r[:half, frame:] * r[:half, frame:] + r[half:, frame:] * r[half:, frame:],
                ],
                axis=0,
            )

        sorted_cols = jnp.dot(
            cat(split_exact(amplitude[slot]), axis=1), stacked(5, 5, 0), preferred_element_type=F32
        )
        sorted_all = jnp.dot(
            stacked(4, 4, 1), cat(split_exact(sorted_cols), axis=0), preferred_element_type=F32
        )
        scale = sorted_all * lax.rsqrt(jnp.maximum(accum[2], INTENSITY_FLOOR))
        ratio[:half, :frame] = scale[:half]
        ratio[half:, :frame] = scale[:half]
        ratio[:half, frame:] = scale[half:]
        ratio[half:, frame:] = scale[half:]
        for part in range(3):
            accum[2 + part] = jnp.zeros((frame, frame), F32)

        @pl.loop(0, modes, unroll=UNROLL)
        def _(m):
            r = left_dot(stacked(0, 1, 1), spectra[m] * ratio[...])
            c, s = turns[0, :half], turns[1, :half]
            er, ei, dr, di = r[:half, :frame], r[half:, :frame], r[:half, frame:], r[half:, frame:]
            vr, vi = dr * c + di * s, di * c - dr * s
            yr = cat([er + vr, er - vr], axis=0)
            yi = cat([ei + vi, ei - vi], axis=0)
            x = cat(
                [cat([yr[:, :half], yi[:, :half]], axis=1), cat([yr[:, half:], yi[:, half:]], axis=1)],
                axis=0,
            )
            y = right_dot(x, stacked(2, 3, 0))
            c, s = turns[0, half : half + 1, :half], turns[1, half : half + 1, :half]
            er, ei, dr, di = y[:frame, :half], y[:frame, half:], y[frame:, :half], y[frame:, half:]
            vr, vi = dr * c + di * s, di * c - dr * s
            qr, qi, pr, pi = accum[0], accum[1], probe[0, m], probe[1, m]
            br = (cat([er + vr, er - vr], axis=1) - (pr * qr - pi * qi)) * flag
            bi = (cat([ei + vi, ei - vi], axis=1) - (pr * qi + pi * qr)) * flag
            accum[2] += pr * br + pi * bi
            accum[3] += pr * bi - pi * br
            accum[4] += flag * (pr * pr + pi * pi)
            gr, gi = qr * br + qi * bi, qr * bi - qi * br
            put(m, gr, slot == 0)
            put(modes + m, gi, slot == 0)

        strength = flag * (qr * qr + qi * qi)
        put(2 * modes, strength, slot == 0)
        for part in range(3):
            piece = accum[2 + part]
            piece = cat([piece, jnp.zeros((frame, width - frame), F32)], axis=1)
            piece = pltpu.roll(piece, col, 1)
            piece = cat([piece, jnp.zeros((height - frame, width), F32)], axis=0)
            piece = pltpu.roll(piece, row, 0)
            totals[part] = piece if slot == 0 else totals[part] + piece


def waves(place, live, own, right, down, diag, probe, amplitude, chunks):
    modes, frame = probe.shape[1], probe.shape[2]
    tile = own.shape[1]
    smem = pl.BlockSpec(memory_space=pltpu.SMEM)
    vmem = pl.BlockSpec(memory_space=pltpu.VMEM)
    return pl.pallas_call(
        waves_kernel,
        out_shape=(
            jax.ShapeDtypeStruct((3, 2 * tile, 2 * tile), F32),
            jax.ShapeDtypeStruct((chunks, 8, 128), F32),
        ),
        in_specs=[smem] * 2 + [vmem] * 8,
        out_specs=(vmem, vmem),
        scratch_shapes=[
            pltpu.VMEM((modes, frame, 2 * frame), F32),
            pltpu.VMEM((frame, 2 * frame), F32),
            pltpu.VMEM((5, frame, frame), F32),
        ],
        compiler_params=pltpu.CompilerParams(vmem_limit_bytes=48 << 20),
        cost_estimate=pl.CostEstimate(
            flops=60_000_000_000, bytes_accessed=16 << 20, transcendentals=0
        ),
    )(place, live, own, right, down, diag, probe, amplitude, *tables(frame))


def moved(value, down, right):
    rows, cols = lax.axis_size("row"), lax.axis_size("col")
    pairs = [
        (r * cols + c, (r + down) * cols + c + right)
        for r in range(rows)
        for c in range(cols)
        if 0 <= r + down < rows and 0 <= c + right < cols
    ]
    return lax.ppermute(value, ("row", "col"), pairs)


def exchange_kernel(
    rows, cols, parts, grad, totals, own, probe, new_object, new_probe,
    acc, inbox, full, fallen, wide, pushed, upd, row_edges, col_edges, inverse,
    send_sem, recv_sem, quad_send, quad_recv, edge_send, edge_recv,
):
    r, c = lax.axis_index("row"), lax.axis_index("col")
    tile = own.shape[1]
    modes, frame = probe.shape[1], probe.shape[2]
    row_bits, col_bits = rows.bit_length() - 1, cols.bit_length() - 1
    core = [(0, bit) for bit in range(row_bits)][:1]
    far = [(0, bit) for bit in range(row_bits)][1:]
    low = [(1, bit) for bit in range(col_bits // 2)]
    high = [(1, bit) for bit in range(col_bits // 2, col_bits)]
    orders = [core + far + low + high, core + low + high + far, core + high + far + low]
    orders = [orders[k % 3] for k in range(len(parts))]
    stages = row_bits + col_bits

    def partner(axis, bit):
        step = 1 << bit
        mine = (c if axis else r) // step % 2
        shift = step - 2 * step * mine
        return mine, ((r, c + shift) if axis else (r + shift, c))

    def near(dr, dc):
        good = jnp.bool_(True)
        if dr > 0:
            good = jnp.logical_and(good, r < rows - dr)
        if dr < 0:
            good = jnp.logical_and(good, r >= -dr)
        if dc > 0:
            good = jnp.logical_and(good, c < cols - dc)
        if dc < 0:
            good = jnp.logical_and(good, c >= -dc)
        return good, (r + dr, c + dc)

    row_edges[...] = jnp.zeros_like(row_edges)
    col_edges[...] = jnp.zeros_like(col_edges)
    barrier = pltpu.get_barrier_semaphore()
    for axis, bit in orders[0]:
        pl.semaphore_signal(
            barrier, inc=1, device_id=partner(axis, bit)[1], device_id_type=pl.DeviceIdType.MESH
        )
    expected = jnp.int32(stages)
    for dr, dc in ((0, 1), (1, 0), (0, -1), (-1, 0)):
        good, there = near(dr, dc)

        @pl.when(good)
        def _():
            pl.semaphore_signal(
                barrier, inc=1, device_id=there, device_id_type=pl.DeviceIdType.MESH
            )

        expected = expected + jnp.where(good, 1, 0)
    pl.semaphore_wait(barrier, expected)

    def remote(source, target, send, recv, there):
        return pltpu.make_async_remote_copy(
            src_ref=source, dst_ref=target, send_sem=send, recv_sem=recv,
            device_id=there, device_id_type=pl.DeviceIdType.MESH,
        )

    ranges = [[start] for start in parts]
    slots = [0]
    copies = {}

    def halve(p, stage):
        start, size = ranges[p][stage]
        mine, there = partner(*orders[p][stage])
        half = size // 2
        box = pl.ds(slots[0], half)
        slots[0] += half
        source = (grad if stage == 0 else acc).at[pl.ds(start + (1 - mine) * half, half)]
        copy = remote(
            source, inbox.at[box], send_sem.at[0, p, stage], recv_sem.at[0, p, stage], there
        )
        copy.start()
        ranges[p].append((start + mine * half, half))
        copies[p, stage] = (copy, box)

    def add(p, stage):
        copy, box = copies[p, stage]
        copy.wait()
        keep = pl.ds(*ranges[p][stage + 1])
        target = full if stage + 1 == stages else acc
        target[keep] = (grad if stage == 0 else acc)[keep] + inbox[box]

    def spread(p, stage):
        there = partner(*orders[p][stage])[1]
        keep = pl.ds(*ranges[p][stage + 1])
        copy = remote(
            full.at[keep], full.at[keep], send_sem.at[1, p, stage], recv_sem.at[1, p, stage], there
        )
        copy.start()
        copies[p, stage] = (copy, None)

    every = range(len(parts))
    for p in every:
        halve(p, 0)
    def send_down():
        good, there = near(1, 0)
        copy = remote(
            totals.at[:, pl.ds(tile, tile)], fallen, quad_send.at[0], quad_recv.at[0], there
        )
        pl.when(good)(copy.start)
        return good, near(-1, 0)[0], copy

    def send_right(good, gets, copy):
        wide[...] = totals[:, :tile]
        pl.when(good)(copy.wait_send)

        @pl.when(gets)
        def _():
            copy.wait_recv()
            wide[...] += fallen[...]

        good, there = near(0, 1)
        copy = remote(
            wide.at[:, :, pl.ds(tile, tile)], pushed, quad_send.at[1], quad_recv.at[1], there
        )
        pl.when(good)(copy.start)
        return good, near(0, -1)[0], copy

    sideways = send_down()
    for stage in range(stages):
        for p in every:
            add(p, stage)
            if stage + 1 < stages:
                halve(p, stage + 1)
            else:
                spread(p, stage)
        if stage == min(1, stages - 1):
            sideways = send_right(*sideways)

    def update():
        good, gets, copy = sideways
        upd[...] = wide[:, :, :tile]
        pl.when(good)(copy.wait_send)

        @pl.when(gets)
        def _():
            copy.wait_recv()
            upd[...] += pushed[...]

        below = upd[2] + OBJECT_DELTA
        upd[0] = own[0] + upd[0] / below
        upd[1] = own[1] + upd[1] / below
        borders = (
            ((1, 0), upd.at[:2, pl.ds(tile - 8, 8)], row_edges.at[0]),
            ((-1, 0), upd.at[:2, pl.ds(0, 8)], row_edges.at[1]),
            ((0, 1), upd.at[:2, :, pl.ds(tile - 128, 128)], col_edges.at[0]),
            ((0, -1), upd.at[:2, :, pl.ds(0, 128)], col_edges.at[1]),
        )
        edges = []
        for k, ((dr, dc), source, target) in enumerate(borders):
            good, there = near(dr, dc)
            copy = remote(source, target, edge_send.at[k], edge_recv.at[k], there)
            pl.when(good)(copy.start)
            edges.append((good, near(-dr, -dc)[0], copy))
        return edges

    def smooth(edges):
        for good, gets, copy in edges:
            pl.when(good)(copy.wait_send)
            pl.when(gets)(copy.wait_recv)
        for part in range(2):
            value = upd[part]
            above, below = row_edges[0, part, 7:8], row_edges[1, part, 0:1]
            before, after = col_edges[0, part][:, 127:128], col_edges[1, part][:, 0:1]
            neighbours = (
                jnp.concatenate([value[1:], below], axis=0)
                + jnp.concatenate([above, value[:-1]], axis=0)
                + jnp.concatenate([value[:, 1:], after], axis=1)
                + jnp.concatenate([before, value[:, :-1]], axis=1)
            )
            new_object[part] = value + SMOOTH_WEIGHT * (neighbours - 4.0 * value)

    update_at, smooth_at = min(2, stages - 1), min(1, stages - 1)
    edges = None
    for stage in reversed(range(stages)):
        for p in every:
            copies[p, stage][0].wait()
            if stage > 0:
                spread(p, stage - 1)
        if stage == update_at:
            edges = update()
        if stage == smooth_at:
            smooth(edges)

    blocks = frame // 8
    for part in range(frame // 128):
        lanes = pl.ds(part * 128, 128)

        def plane(index):
            where = pl.ds((index * (frame // 128) + part) * blocks, blocks)
            return full[where].reshape(frame, 128)

        inverse[...] = 1.0 / (plane(2 * modes) + PROBE_DELTA)

        @pl.loop(0, modes)
        def _(m):
            new_probe[0, m, :, lanes] = probe[0, m, :, lanes] + plane(m) * inverse[...]
            new_probe[1, m, :, lanes] = probe[1, m, :, lanes] + plane(modes + m) * inverse[...]


def cut(probe, devices):
    modes, frame = probe.shape[1], probe.shape[2]
    used = (2 * modes + 1) * (frame // 128) * (frame // 8)
    units = -(-used // devices)
    bounds = [units * k // 6 * devices for k in range(7)]
    return units * devices, [(a, b - a) for a, b in zip(bounds, bounds[1:]) if b > a]


def exchange(grad, totals, own, probe, parts):
    rows, cols = lax.axis_size("row"), lax.axis_size("col")
    frame, tile = probe.shape[2], own.shape[1]
    stages = (rows * cols).bit_length() - 1
    vmem = pl.BlockSpec(memory_space=pltpu.VMEM)
    dma = pltpu.SemaphoreType.DMA
    return pl.pallas_call(
        functools.partial(exchange_kernel, rows, cols, parts),
        out_shape=(
            jax.ShapeDtypeStruct(own.shape, F32),
            jax.ShapeDtypeStruct(probe.shape, F32),
        ),
        in_specs=[vmem] * 4,
        out_specs=(vmem, vmem),
        scratch_shapes=[
            pltpu.VMEM(grad.shape, F32),
            pltpu.VMEM(grad.shape, F32),
            pltpu.VMEM(grad.shape, F32),
            pltpu.VMEM((3, tile, 2 * tile), F32),
            pltpu.VMEM((3, tile, 2 * tile), F32),
            pltpu.VMEM((3, tile, tile), F32),
            pltpu.VMEM((3, tile, tile), F32),
            pltpu.VMEM((2, 2, 8, tile), F32),
            pltpu.VMEM((2, 2, tile, 128), F32),
            pltpu.VMEM((frame, 128), F32),
            dma((2, len(parts), stages)),
            dma((2, len(parts), stages)),
            dma((2,)),
            dma((2,)),
            dma((4,)),
            dma((4,)),
        ],
        compiler_params=pltpu.CompilerParams(
            vmem_limit_bytes=48 << 20, collective_id=0, has_side_effects=True
        ),
        cost_estimate=pl.CostEstimate(flops=1 << 22, bytes_accessed=24 << 20, transcendentals=0),
    )(grad, totals, own, probe)


def per_device(object_field, probe_modes, patterns, offsets, counts):
    tile, frame = object_field.shape[1], probe_modes.shape[-1]
    slots = patterns.shape[0]
    right = moved(object_field, 0, -1)
    down = moved(object_field, -1, 0)
    diag = moved(right, -1, 0)
    base = jnp.stack([lax.axis_index("row"), lax.axis_index("col")]).astype(jnp.int32) * tile
    place = offsets - base[:, None]
    live = (jnp.arange(slots, dtype=jnp.int32) < counts[0]).astype(jnp.int32)
    chunks, parts = cut(probe_modes, lax.axis_size("row") * lax.axis_size("col"))
    totals, gradient = waves(
        place, live, object_field, right, down, diag, probe_modes, patterns, chunks
    )
    return exchange(gradient, totals, object_field, probe_modes, parts)


def solution(mesh):
    return jax.shard_map(
        per_device,
        mesh=mesh,
        in_specs=(
            P(None, "row", "col"),
            P(),
            P(("row", "col"), None, None),
            P(None, ("row", "col")),
            P(("row", "col")),
        ),
        out_specs=(P(None, "row", "col"), P()),
        check_vma=False,
    )
```
